128 devices in a mesh: row: 8 (over x, z_lo), col: 16 (over z_hi, y, core).
Axes of the slice: x: 4, y: 4, z: 4 (z_hi: 2, z_lo: 2; z = z_hi * 2 + z_lo), core: 2. Of those that a mesh axis runs over, the one named last changes fastest.
Arguments:
- inputs: bfloat16 [2048, 16384], P('col', 'row'), may hold values from -0.25 to 0.25
- weight: bfloat16 [16384, 18432], P('row', 'col'), may hold values from -0.046875 to 0.046875
- out_grad: bfloat16 [2048, 18432], P('row', 'col'), may hold values from -3 to 3
Outputs:
- input_grad: bfloat16 [2048, 16384], P('col', 'row')
- weight_grad: float32 [16384, 18432], P('row', 'col')
The draws below stay inside these ranges and needn't reach their ends.
All inputs are finite; a program needn't handle non-finite values.
Results may differ from the reference program's by a relative error of at most 0.019.
Values may be sent and summed in bfloat16 or wider, within the bound.
No kernel may reach another device: no remote copies, remote signals or barrier semaphores. Data moves between devices by JAX's collectives and lax.ppermute only.
A program may use at most 128 MiB of HBM per device.

```python
import jax
import jax.numpy as jnp
from jax import lax

D = 16384
E = 18432
TOKENS = 2048
N_COL = 16


def raised(drawn, stream_key, source, target, blocks, factor):
    owner, partner = [(jnp.arange(drawn.shape[position]) // (drawn.shape[position] // blocks)).reshape([-1 if axis == position else 1 for axis in range(drawn.ndim)]) for position in (source, target)]
    chosen = jax.random.permutation(stream_key, blocks)[partner]
    strong = (owner == chosen) | (owner == (partner + blocks // 2) % blocks)
    return jnp.where(strong, factor * drawn, drawn)


def steps_of(own_key, extent, split, least, high):
    gain, own = 1.0, jax.random.fold_in(own_key, 6)
    for axis_at, shards_of in split:
        draws = jnp.exp(jax.random.uniform(jax.random.fold_in(own, axis_at), (shards_of,), jnp.float32, least / len(split), high / len(split)))
        gain = gain * jnp.repeat(draws, extent[axis_at] // shards_of).reshape([-1 if axis == axis_at else 1 for axis in range(len(extent))])
    return gain


def gaussian(stream_key, extent, width, bound, cuts=(), dtype=jnp.bfloat16):
    gain = steps_of(stream_key, extent, cuts, -0.22, 0.18) if cuts else 1.0
    drawn = jax.random.normal(stream_key, extent, jnp.float32) * width * gain
    return jnp.minimum(jnp.maximum(drawn, -bound), bound).astype(dtype)


def noise_with(own_key, shape, spread, most, cuts, heavy, held_as=jnp.bfloat16):
    result = spread * jax.random.normal(own_key, shape, jnp.float32)
    if cuts:
        result = result * steps_of(own_key, shape, cuts, -0.22, 0.18)
    return jnp.clip(raised(result, jax.random.fold_in(own_key, 3), *heavy), -most, most).astype(held_as)


def setup_inputs(seed: int = 0) -> dict:
    splits = jax.random.split(jax.random.key(seed), 4)
    inputs = gaussian(splits[0], (TOKENS, D), (TOKENS // 4) ** -0.5, 0.25, ((0, 16), (1, 8)))
    weight = gaussian(splits[1], (D, E), D ** -0.5, 0.046875, ((0, 8), (1, 16)))
    out_grad = noise_with(splits[2], (TOKENS, E), 0.5, 3.0, ((0, 8), (1, 16)), (1, 0, 16, 2.0))
    return {"inputs": inputs, "weight": weight, "out_grad": out_grad}


def reference(inputs, weight, out_grad):
    block = E // N_COL
    grad_blocks = out_grad.reshape(out_grad.shape[0], N_COL, block).transpose(1, 0, 2)
    weight_blocks = weight.reshape(weight.shape[0], N_COL, block).transpose(1, 0, 2)

    def add_block(total, pair):
        grads, weights = pair
        term = lax.dot_general(grads, weights, (((1,), (1,)), ((), ())), preferred_element_type=jnp.float32)
        return total + term.astype(jnp.bfloat16).astype(jnp.float32), None

    empty = jnp.zeros((out_grad.shape[0], weight.shape[0]), jnp.float32)
    input_grad, unused = lax.scan(add_block, empty, (grad_blocks, weight_blocks))
    weight_grad = lax.dot_general(inputs, out_grad, (((0,), (0,)), ((), ())), preferred_element_type=jnp.float32)
    return input_grad.astype(jnp.bfloat16), weight_grad
```

```python
import jax
import jax.numpy as jnp
from jax import lax
from jax.sharding import Mesh
from jax.sharding import PartitionSpec as P

AXES = ("x", "zl", "zh", "y", "core")
SIZES = (4, 2, 2, 4, 2)


def shift(value, axis, step):
    return lax.ppermute(value, axis, [(i, (i + step) % 4) for i in range(4)])


def swap(value, axis):
    return lax.ppermute(value, axis, [(0, 1), (1, 0)])


def after(value, *others):
    return lax.optimization_barrier((value, *others))[0]


def dot_nt(a, b):
    return lax.dot_general(a, b, (((1,), (1,)), ((), ())), preferred_element_type=jnp.float32)


def on_device(inputs, weight, out_grad):
    bf16, f32 = jnp.bfloat16, jnp.float32
    x, zl, zh, y, core = (lax.axis_index(axis) for axis in AXES)

    g = out_grad
    g1, g3, g2 = shift(g, "x", 1), shift(g, "x", -1), shift(g, "x", 2)
    h = swap(g, "zl")
    h1, h3 = shift(h, "x", 1), shift(h, "x", -1)
    h2 = swap(g2, "zl")

    a = inputs
    a1 = shift(a, "y", 1)
    a3 = shift(after(a, a1), "y", -1)
    b = swap(after(a, h), "zh")
    a2 = shift(after(a, a3), "y", 2)
    b1 = shift(after(b, h1), "y", 1)
    b3 = shift(after(b, a2), "y", -1)
    b2 = shift(after(b, b1), "y", 2)

    grads = jnp.zeros((2, 8, 128, 1152), bf16)
    for block, dx, dz in ((g, 0, 0), (g1, 3, 0), (g3, 1, 0), (g2, 2, 0), (h, 0, 1), (h1, 3, 1), (h3, 1, 1), (h2, 2, 1)):
        bx, bz = (x + dx) & 3, zl ^ dz
        slot = (zh ^ (bx >> 1)) * 4 + ((((bx & 1) << 1) + bz - y) & 3)
        block = block.reshape(2, 1, 1, 128, 1152)
        for dc in range(2):
            half = lax.dynamic_index_in_dim(block, core ^ dc, 0, keepdims=False)
            grads = lax.dynamic_update_slice(grads, half, (dc, slot, 0, 0))
    mine, theirs = grads[0].reshape(1024, 1152), grads[1].reshape(1024, 1152)

    def partial(w):
        other = swap(dot_nt(theirs, w).astype(bf16), "core")
        return (dot_nt(mine, w) + other.astype(f32)).astype(bf16).reshape(2, 4, 128, 1024)

    def over_y(p):
        return p[:, 0], shift(p[:, 1], "y", 1), shift(p[:, 3], "y", -1), shift(p[:, 2], "y", 2)

    def over_zh(p):
        return p[0], swap(p[1], "zh")

    def total(parts):
        return sum(part.astype(f32) for part in parts)

    pa, pb = partial(weight[:1024]), partial(weight[1024:])
    sa, sb = over_y(pa), over_zh(pb)

    own = jnp.concatenate([a, a3, a2, a1, b, b3, b2, b1], axis=0)
    own = after(own, pb)
    tokens = jnp.concatenate([own, swap(own, "core")], axis=0)
    weight_grad = lax.dot_general(
        tokens, grads.reshape(2048, 1152), (((0,), (0,)), ((), ())), preferred_element_type=f32
    )

    sa, sb, weight_grad = lax.optimization_barrier((sa, sb, weight_grad))
    sa, sb = over_zh(total(sa).astype(bf16)), over_y(total(sb).astype(bf16)[None])
    input_grad = jnp.concatenate([total(sa), total(sb)[0]], axis=1).astype(bf16)
    return input_grad, weight_grad


def solution(mesh):
    fine = Mesh(mesh.devices.reshape(SIZES), AXES)
    row, col = ("x", "zl"), ("zh", "y", "core")
    return jax.shard_map(
        on_device,
        mesh=fine,
        in_specs=(P(col, row), P(row, col), P(row, col)),
        out_specs=(P(col, row), P(row, col)),
        check_vma=False,
    )
```

```python
import jax
import jax.numpy as jnp
from jax import lax
from jax.experimental import pallas as pl
from jax.experimental.pallas import tpu as pltpu
from jax.experimental.layout import Layout, with_layout_constraint
from jax.sharding import Mesh
from jax.sharding import PartitionSpec as P

AXES = ("x", "zl", "zh", "y", "core")
SIZES = (4, 2, 2, 4, 2)


def shift(value, axis, step):
    return lax.ppermute(value, axis, [(i, (i + step) % 4) for i in range(4)])


def swap(value, axis):
    return lax.ppermute(value, axis, [(0, 1), (1, 0)])


def after(value, *others):
    return lax.optimization_barrier((value, *others))[0]


def dot_nt(a, b):
    return lax.dot_general(a, b, (((1,), (1,)), ((), ())), preferred_element_type=jnp.float32)


def dot_tn(a, b):
    return lax.dot_general(a, b, (((0,), (0,)), ((), ())), preferred_element_type=jnp.float32)


def kernel_of(kernel, name, operands, shapes, waits=()):
    whole, anywhere = pl.BlockSpec(), pl.BlockSpec(memory_space=pl.ANY)
    n = len(operands)
    return pl.pallas_call(
        lambda *refs: kernel(*refs[:n], *refs[n + len(waits) :]),
        name=name,
        out_shape=[jax.ShapeDtypeStruct(shape, jnp.bfloat16) for shape in shapes],
        in_specs=[whole] * n + [anywhere] * len(waits),
        out_specs=[whole] * len(shapes),
        compiler_params=pltpu.CompilerParams(vmem_limit_bytes=16 * 2**20),
    )(*operands, *waits)


def place_grads(g0, g1, g2, g3, h0, h1, h2, h3, mine, theirs, *parts):
    x, zl, zh, y, core = (lax.axis_index(axis) for axis in AXES)
    for i, block in enumerate((g0, g1, g2, g3, h0, h1, h2, h3)):
        bx, bz = (x + i) & 3, zl ^ (i >> 2)
        dz, dy = zh ^ (bx >> 1), (((bx & 1) << 1) + bz - y) & 3
        first = block[pl.ds(pl.multiple_of(core * 128, 128), 128)]
        second = block[pl.ds(pl.multiple_of(128 - core * 128, 128), 128)]
        mine[dz * 4 + dy] = first
        theirs[dz * 4 + dy] = second
        for at in range(2):

            @pl.when(dz == at)
            def _():
                parts[at][dy] = first
                parts[2 + at][dy] = second


def sum_blocks(first, second, *outs):
    for i, out in enumerate(outs):
        out[...] = (first[i].astype(jnp.float32) + second[i].astype(jnp.float32)).astype(jnp.bfloat16)


def sum_four(q0, q1, q2, q3, *outs):
    for i, out in enumerate(outs):
        total = sum(q[i].astype(jnp.float32) for q in (q0, q1, q2, q3))
        out[...] = total.astype(jnp.bfloat16)


def sum_last(a0, a1, b0, b1, b2, b3, out):
    f32 = jnp.float32
    out[:, :1024] = (a0[...].astype(f32) + a1[...].astype(f32)).astype(jnp.bfloat16)
    total = b0[...].astype(f32) + b1[...].astype(f32) + b2[...].astype(f32) + b3[...].astype(f32)
    out[:, 1024:] = total.astype(jnp.bfloat16)


def relay(block, out):
    out[...] = block[...]


def pair(a, b, out):
    out[0] = a[...]
    out[1] = b[...]


def halves(behind, ahead, first, second):
    first[...] = behind[:, :64]
    second[...] = ahead[:, 64:]


def near_first(ab, ahead, behind, first, second, out):
    for dz in range(2):
        out[dz * 4] = ab[dz]
        out[dz * 4 + 1] = ahead[dz]
        out[dz * 4 + 2, :64] = first[dz]
        out[dz * 4 + 2, 64:] = second[dz]
        out[dz * 4 + 3] = behind[dz]


def cut(p, *outs):
    for i, out in enumerate(outs):
        out[...] = p[:, i]


def on_device(inputs, weight, out_grad):
    bf16, f32 = jnp.bfloat16, jnp.float32

    g, h = out_grad, swap(out_grad, "zl")
    g1, g3, g2 = shift(g, "x", 1), shift(g, "x", -1), shift(g, "x", 2)

    (ab,) = kernel_of(pair, "pair", (inputs, swap(inputs, "zh")), [(2, 128, 2048)])
    behind, ahead = shift(ab, "y", 1), shift(ab, "y", -1)
    first, second = kernel_of(halves, "halves", (behind, ahead), [(2, 64, 2048)] * 2)

    (h,) = kernel_of(relay, "relay", (h,), [(256, 1152)], (ab, g1, g3))
    h1, h3, h2 = shift(h, "x", 1), shift(h, "x", -1), swap(g2, "zl")
    blocks = [(8, 128, 1152)] * 2 + [(4, 128, 1152)] * 4
    grads = kernel_of(place_grads, "place_grads", (g, g3, g2, g1, h, h3, h2, h1), blocks, (first,))
    mine, theirs, mine_near, mine_far, theirs_near, theirs_far = (part.reshape(-1, 1152) for part in grads)

    wa, wb = weight[:1024], weight[1024:]

    def partial(rows, w, part):
        return (dot_nt(rows, w) + part.astype(f32)).astype(bf16).reshape(-1, 4, 128, 1024)

    tb1 = dot_nt(theirs_far, wb).astype(bf16)
    ta = dot_nt(after(theirs, tb1), wa).astype(bf16)
    pb1 = partial(mine_far, wb, swap(tb1, "core"))
    pa = partial(after(mine, pb1), wa, swap(ta, "core"))
    qb = swap(pb1[0], "zh")
    q0, q1, q2, q3 = kernel_of(cut, "cut", (pa,), [(2, 128, 1024)] * 4)
    q1, q3, q2 = shift(q1, "y", 1), shift(q3, "y", -1), shift(q2, "y", 2)
    tb0 = dot_nt(theirs_near, wb).astype(bf16)
    pb0 = partial(mine_near, wb, swap(tb0, "core"))

    first, second = shift(first, "y", 1), shift(second, "y", -1)
    waits = (q1, q2, q3, first, second)
    s0, s1, s2, s3 = kernel_of(sum_blocks, "sum_zh", (pb0[0], qb), [(128, 1024)] * 4, waits)
    r1, r3, r2 = shift(s1, "y", 1), shift(s3, "y", -1), shift(s2, "y", 2)
    a0, a1 = kernel_of(sum_four, "sum_y", (q0, q1, q2, q3), [(128, 1024)] * 2)
    a1 = swap(a1, "zh")

    (own,) = kernel_of(near_first, "near_first", (ab, ahead, behind, first, second), [(8, 128, 2048)], (s1, a1))
    own = own.reshape(1024, 2048)
    weight_grad = dot_tn(own, mine) + dot_tn(swap(own, "core"), theirs)
    weight_grad = with_layout_constraint(weight_grad, Layout((0, 1)))

    parts = (a0, a1, s0, r1, r3, r2)
    (input_grad,) = kernel_of(sum_last, "sum_last", parts, [(128, 2048)], (weight_grad,))
    return input_grad, weight_grad


def solution(mesh):
    fine = Mesh(mesh.devices.reshape(SIZES), AXES)
    row, col = ("x", "zl"), ("zh", "y", "core")
    return jax.shard_map(
        on_device,
        mesh=fine,
        in_specs=(P(col, row), P(row, col), P(row, col)),
        out_specs=(P(col, row), P(row, col)),
        check_vma=False,
    )
```

```python
import jax
import jax.numpy as jnp
from jax import lax
from jax.experimental import pallas as pl
from jax.experimental.pallas import tpu as pltpu
from jax.experimental.layout import Layout, with_layout_constraint
from jax.sharding import Mesh
from jax.sharding import PartitionSpec as P

AXES = ("x", "zl", "zh", "y", "core")
SIZES = (4, 2, 2, 4, 2)


def shift(value, axis, step):
    return lax.ppermute(value, axis, [(i, (i + step) % 4) for i in range(4)])


def swap(value, axis):
    return lax.ppermute(value, axis, [(0, 1), (1, 0)])


def after(value, *others):
    return lax.optimization_barrier((value, *others))[0]


def dot_nt(a, b):
    return lax.dot_general(a, b, (((1,), (1,)), ((), ())), preferred_element_type=jnp.float32)


def dot_tn(a, b):
    return lax.dot_general(a, b, (((0,), (0,)), ((), ())), preferred_element_type=jnp.float32)


def kernel_of(kernel, name, operands, shapes, waits=()):
    whole, anywhere = pl.BlockSpec(), pl.BlockSpec(memory_space=pl.ANY)
    n = len(operands)
    return pl.pallas_call(
        lambda *refs: kernel(*refs[:n], *refs[n + len(waits) :]),
        name=name,
        out_shape=[jax.ShapeDtypeStruct(shape, jnp.bfloat16) for shape in shapes],
        in_specs=[whole] * n + [anywhere] * len(waits),
        out_specs=[whole] * len(shapes),
        compiler_params=pltpu.CompilerParams(vmem_limit_bytes=16 * 2**20),
    )(*operands, *waits)


def distance(dx, dz):
    x, zl, zh, y = (lax.axis_index(axis) for axis in AXES[:4])
    bx, bz = (x + dx) & 3, zl ^ dz
    return zh ^ (bx >> 1), (((bx & 1) << 1) + bz - y) & 3


def by_core(*refs):
    core = lax.axis_index("core")
    for i, block in enumerate(refs[:4]):
        refs[4][i] = block[pl.ds(pl.multiple_of(core * 128, 128), 128)]
        refs[5][i] = block[pl.ds(pl.multiple_of(128 - core * 128, 128), 128)]


def place_grads(early_mine, early_theirs, late_mine, late_theirs, mine, theirs, mine_opposite, theirs_opposite):
    for late, part, other in ((0, early_mine, early_theirs), (1, late_mine, late_theirs)):
        for i in range(4):
            dz, dy = distance(i, late)

            @pl.when(dy == 2)
            def _():
                mine_opposite[dz] = part[i]
                theirs_opposite[dz] = other[i]

            @pl.when(dy != 2)
            def _():
                mine[dz * 3 + dy - (dy >> 1)] = part[i]
                theirs[dz * 3 + dy - (dy >> 1)] = other[i]


def cut_a(early, late, first, second, q0, q1, q2, q3):
    for is_late, part in ((0, early), (1, late)):
        for i in range(4):
            dz, dy = distance(i, is_late)
            for at, out in enumerate((q0, q1, q2, q3)):

                @pl.when(dy == at)
                def _():
                    out[dz] = part[i, :, :1024]

    for out, half in ((q1, first), (q3, second)):
        for dz in range(2):
            out[2 + dz, :64] = half[dz, :, :1024]
            out[2 + dz, 64:] = half[dz, :, 1024:]


def cut_b(early, late, near, far):
    for is_late, part, columns in ((0, early, slice(1024, 2048)), (1, late, slice(0, 1024))):
        for i in range(4):
            dz, dy = distance(i, is_late)
            for at, out in enumerate((near, far)):

                @pl.when(dz == at)
                def _():
                    out[dy] = part[i, :, columns]


def sum_blocks(first, second, *outs):
    for i, out in enumerate(outs):
        out[...] = (first[i].astype(jnp.float32) + second[i].astype(jnp.float32)).astype(jnp.bfloat16)


def sum_four(q0, q1, q2, q3, *outs):
    for i, out in enumerate(outs):
        total = sum(q[i].astype(jnp.float32) for q in (q0, q1, q2, q3))
        out[...] = total.astype(jnp.bfloat16)


def sum_last(a0, a1, b0, b1, b2, b3, out):
    f32 = jnp.float32
    out[:, :1024] = (a0[...].astype(f32) + a1[...].astype(f32)).astype(jnp.bfloat16)
    total = b0[...].astype(f32) + b1[...].astype(f32) + b2[...].astype(f32) + b3[...].astype(f32)
    out[:, 1024:] = total.astype(jnp.bfloat16)


def relay(block, out):
    out[...] = block[...]


def pair(a, b, out):
    out[0] = a[...]
    out[1] = b[...]


def halves(behind, ahead, first, second):
    first[...] = behind[:, :64]
    second[...] = ahead[:, 64:]


def near_first(ab, ahead, behind, out):
    for dz in range(2):
        for i, block in enumerate((ab, ahead, behind)):
            out[dz * 3 + i] = block[dz]


def opposite(behind, ahead, out):
    for rows, half in ((slice(0, 64), behind), (slice(64, 128), ahead)):
        for dz in range(2):
            out[dz, rows, :1024] = half[2 + dz, :64]
            out[dz, rows, 1024:] = half[2 + dz, 64:]


def pair_up(a0, a1, b0, b1, a, b):
    for out, parts in ((a, (a0, a1)), (b, (b0, b1))):
        for i, part in enumerate(parts):
            out[2 * i] = part[0]
            out[2 * i + 1] = part[1]


def on_device(inputs, weight, out_grad):
    bf16, f32 = jnp.bfloat16, jnp.float32

    g, h = out_grad, swap(out_grad, "zl")
    g2 = shift(g, "x", 2)

    (ab,) = kernel_of(pair, "pair", (inputs, swap(inputs, "zh")), [(2, 128, 2048)])
    (g,) = kernel_of(relay, "relay_g", (g,), [(256, 1152)], (g2, ab))
    g1, g3 = shift(g, "x", 1), shift(g, "x", -1)
    behind, ahead = shift(ab, "y", 1), shift(ab, "y", -1)
    first, second = kernel_of(halves, "halves", (behind, ahead), [(2, 64, 2048)] * 2)

    (h,) = kernel_of(relay, "relay", (h,), [(256, 1152)], (ab, g1, g3))
    h1, h3, h2 = shift(h, "x", 1), shift(h, "x", -1), swap(g2, "zl")
    wa, wb = weight[:1024], weight[1024:]
    blocks = [(4, 128, 1152)] * 2
    early_mine, early_theirs = kernel_of(by_core, "by_core_early", (g, g3, g2, g1), blocks)

    def theirs_of(part, w):
        return dot_nt(part.reshape(512, 1152), w).astype(bf16)

    def partial(part, w, other):
        return (dot_nt(part.reshape(512, 1152), w) + other.astype(f32)).astype(bf16).reshape(4, 128, -1)

    early = partial(early_mine, weight, swap(theirs_of(early_theirs, weight), "core"))
    late_mine, late_theirs = kernel_of(by_core, "by_core_late", (h, h3, h2, h1), blocks, (first,))
    late_b = theirs_of(late_theirs, wb)
    late_a = theirs_of(after(late_theirs, late_b), wa)
    late_b = partial(late_mine, wb, swap(late_b, "core"))
    late_a = partial(after(late_mine, late_b), wa, swap(late_a, "core"))
    near, far = kernel_of(cut_b, "cut_b", (early, late_b), [(4, 128, 1024)] * 2)
    far = swap(far, "zh")
    cuts = [(2, 128, 1024), (4, 128, 1024)] * 2
    q0, q1, q2, q3 = kernel_of(cut_a, "cut_a", (early, late_a, first, second), cuts)
    q1, q3, q2 = shift(q1, "y", 1), shift(q3, "y", -1), shift(q2, "y", 2)

    (own,) = kernel_of(near_first, "near_first", (ab, ahead, behind), [(6, 128, 2048)], (q0,))
    own = own.reshape(768, 2048)
    parts = (early_mine, early_theirs, late_mine, late_theirs)
    grads = kernel_of(place_grads, "place_grads", parts, [(6, 128, 1152)] * 2 + [(2, 128, 1152)] * 2, (q0,))
    mine, theirs = (part.reshape(768, 1152) for part in grads[:2])
    mine_opposite, theirs_opposite = grads[2:]
    weight_grad = dot_tn(own, mine) + dot_tn(swap(own, "core"), theirs)

    waits = (q1, q2, q3, far, weight_grad)
    s0, s1, s2, s3 = kernel_of(sum_blocks, "sum_zh", (near, far), [(128, 1024)] * 4, waits)
    r1, r3, r2 = shift(s1, "y", 1), shift(s3, "y", -1), shift(s2, "y", 2)
    a0, a1 = kernel_of(sum_four, "sum_y", (q0, q1, q2, q3), [(128, 1024)] * 2, waits)
    a1 = swap(a1, "zh")

    (own,) = kernel_of(opposite, "opposite", (q1, q3), [(2, 128, 2048)], (s1,))
    own, other = kernel_of(pair_up, "pair_up", (own, swap(own, "core"), mine_opposite, theirs_opposite), [(4, 128, 2048), (4, 128, 1152)])
    weight_grad += dot_tn(own.reshape(512, 2048), other.reshape(512, 1152))
    weight_grad = with_layout_constraint(weight_grad, Layout((0, 1)))

    parts = (a0, a1, s0, r1, r3, r2)
    (input_grad,) = kernel_of(sum_last, "sum_last", parts, [(128, 2048)], (weight_grad,))
    return input_grad, weight_grad


def solution(mesh):
    fine = Mesh(mesh.devices.reshape(SIZES), AXES)
    row, col = ("x", "zl"), ("zh", "y", "core")
    return jax.shard_map(
        on_device,
        mesh=fine,
        in_specs=(P(col, row), P(row, col), P(row, col)),
        out_specs=(P(col, row), P(row, col)),
        check_vma=False,
    )
```

```python
import jax
import jax.numpy as jnp
from jax import lax
from jax.experimental import pallas as pl
from jax.experimental.pallas import tpu as pltpu
from jax.experimental.layout import Layout, with_layout_constraint
from jax.sharding import Mesh
from jax.sharding import PartitionSpec as P

AXES = ("x", "zl", "zh", "y", "core")
SIZES = (4, 2, 2, 4, 2)


NEAR = 896
PACKED = [((slice(0, 64), slice(512 * i, 512 * i + 512)), (slice(64 * i, 64 * i + 64), slice(0, 512))) for i in range(2)]
PACKED += [((slice(64, 96), slice(256 * i, 256 * i + 256)), (slice(32 * i, 32 * i + 32), slice(512, 768))) for i in range(4)]
PACKED += [((slice(96, 112), slice(128 * i, 128 * i + 128)), (slice(16 * i, 16 * i + 16), slice(768, 896))) for i in range(8)]


def shift(value, axis, step):
    return lax.ppermute(value, axis, [(i, (i + step) % 4) for i in range(4)])


def swap(value, axis):
    return lax.ppermute(value, axis, [(0, 1), (1, 0)])


def after(value, *others):
    return lax.optimization_barrier((value, *others))[0]


def dot_nt(a, b):
    return lax.dot_general(a, b, (((1,), (1,)), ((), ())), preferred_element_type=jnp.float32)


def dot_tn(a, b):
    return lax.dot_general(a, b, (((0,), (0,)), ((), ())), preferred_element_type=jnp.float32)


def kernel_of(kernel, name, operands, shapes, waits=()):
    whole, anywhere = pl.BlockSpec(), pl.BlockSpec(memory_space=pl.ANY)
    n = len(operands)
    return pl.pallas_call(
        lambda *refs: kernel(*refs[:n], *refs[n + len(waits) :]),
        name=name,
        out_shape=[jax.ShapeDtypeStruct(shape, jnp.bfloat16) for shape in shapes],
        in_specs=[whole] * n + [anywhere] * len(waits),
        out_specs=[whole] * len(shapes),
        compiler_params=pltpu.CompilerParams(vmem_limit_bytes=16 * 2**20),
    )(*operands, *waits)


def distance(dx, dz):
    x, zl, zh, y = (lax.axis_index(axis) for axis in AXES[:4])
    bx, bz = (x + dx) & 3, zl ^ dz
    return zh ^ (bx >> 1), (((bx & 1) << 1) + bz - y) & 3


def by_core(*refs):
    core = lax.axis_index("core")
    for i, block in enumerate(refs[:4]):
        refs[4][i] = block[pl.ds(pl.multiple_of(core * 128, 128), 128)]
        refs[5][i] = block[pl.ds(pl.multiple_of(128 - core * 128, 128), 128)]


def place_grads(early_mine, early_theirs, late_mine, late_theirs, mine, theirs, mine_opposite, theirs_opposite):
    for late, part, other in ((0, early_mine, early_theirs), (1, late_mine, late_theirs)):
        for i in range(4):
            dz, dy = distance(i, late)

            @pl.when(dy == 2)
            def _():
                mine_opposite[dz] = part[i]
                theirs_opposite[dz] = other[i]

            @pl.when(dy != 2)
            def _():
                mine[dz * 3 + dy - (dy >> 1)] = part[i]
                theirs[dz * 3 + dy - (dy >> 1)] = other[i]


def cut_a(early, late, first, second, q0, q1, q2, q3):
    for is_late, part in ((0, early), (1, late)):
        for i in range(4):
            dz, dy = distance(i, is_late)
            for at, out in enumerate((q0, q1, q2, q3)):

                @pl.when(dy == at)
                def _():
                    if at % 2 == 0:
                        out[dz] = part[i, :, :NEAR]
                    else:
                        for there, here in PACKED:
                            out[dz, *there] = part[i, *here]

    for out, half in ((q1, first), (q3, second)):
        for dz in range(2):
            out[dz, 112:176] = half[dz, :, :1024]
            out[dz, 176:] = half[dz, :, 1024:]


def cut_b(early, late, near, far):
    for is_late, part, columns in ((0, early, slice(NEAR, 2048)), (1, late, slice(0, 2048 - NEAR))):
        for i in range(4):
            dz, dy = distance(i, is_late)
            for at, out in enumerate((near, far)):

                @pl.when(dz == at)
                def _():
                    out[dy] = part[i, :, columns]


def sum_blocks(first, second, *outs):
    for i, out in enumerate(outs):
        out[...] = (first[i].astype(jnp.float32) + second[i].astype(jnp.float32)).astype(jnp.bfloat16)


def sum_four(q0, q1, q2, q3, *outs):
    for i, out in enumerate(outs):
        for there, here in PACKED:
            total = q0[i, *here].astype(jnp.float32) + q2[i, *here].astype(jnp.float32)
            total += q1[i, *there].astype(jnp.float32) + q3[i, *there].astype(jnp.float32)
            out[here] = total.astype(jnp.bfloat16)


def sum_last(a0, a1, b0, b1, b2, b3, out):
    f32 = jnp.float32
    out[:, :NEAR] = (a0[...].astype(f32) + a1[...].astype(f32)).astype(jnp.bfloat16)
    total = b0[...].astype(f32) + b1[...].astype(f32) + b2[...].astype(f32) + b3[...].astype(f32)
    out[:, NEAR:] = total.astype(jnp.bfloat16)


def relay(block, out):
    out[...] = block[...]


def pair(a, b, out):
    out[0] = a[...]
    out[1] = b[...]


def halves(behind, ahead, first, second):
    first[...] = behind[:, :64]
    second[...] = ahead[:, 64:]


def near_first(ab, ahead, behind, out):
    for dz in range(2):
        for i, block in enumerate((ab, ahead, behind)):
            out[dz * 3 + i] = block[dz]


def opposite(behind, ahead, out):
    for rows, half in ((slice(0, 64), behind), (slice(64, 128), ahead)):
        for dz in range(2):
            out[dz, rows, :1024] = half[dz, 112:176]
            out[dz, rows, 1024:] = half[dz, 176:]


def pair_up(a0, a1, b0, b1, a, b):
    for out, parts in ((a, (a0, a1)), (b, (b0, b1))):
        for i, part in enumerate(parts):
            out[2 * i] = part[0]
            out[2 * i + 1] = part[1]


def on_device(inputs, weight, out_grad):
    bf16, f32 = jnp.bfloat16, jnp.float32

    g, h = out_grad, swap(out_grad, "zl")
    g2 = shift(g, "x", 2)

    (ab,) = kernel_of(pair, "pair", (inputs, swap(inputs, "zh")), [(2, 128, 2048)])
    (g,) = kernel_of(relay, "relay_g", (g,), [(256, 1152)], (g2, ab))
    g1, g3 = shift(g, "x", 1), shift(g, "x", -1)
    behind, ahead = shift(ab, "y", 1), shift(ab, "y", -1)
    first, second = kernel_of(halves, "halves", (behind, ahead), [(2, 64, 2048)] * 2)

    (h,) = kernel_of(relay, "relay", (h,), [(256, 1152)], (ab, g1, g3))
    h1, h3, h2 = shift(h, "x", 1), shift(h, "x", -1), swap(g2, "zl")
    wa, wb = weight[:NEAR], weight[NEAR:]
    blocks = [(4, 128, 1152)] * 2
    early_mine, early_theirs = kernel_of(by_core, "by_core_early", (g, g3, g2, g1), blocks)

    def theirs_of(part, w):
        return dot_nt(part.reshape(512, 1152), w).astype(bf16)

    def partial(part, w, other):
        return (dot_nt(part.reshape(512, 1152), w) + other.astype(f32)).astype(bf16).reshape(4, 128, -1)

    early = partial(early_mine, weight, swap(theirs_of(early_theirs, weight), "core"))
    late_mine, late_theirs = kernel_of(by_core, "by_core_late", (h, h3, h2, h1), blocks, (first,))
    late_b = theirs_of(late_theirs, wb)
    late_a = theirs_of(after(late_theirs, late_b), wa)
    late_b = partial(late_mine, wb, swap(late_b, "core"))
    late_a = partial(after(late_mine, late_b), wa, swap(late_a, "core"))
    near, far = kernel_of(cut_b, "cut_b", (early, late_b), [(4, 128, 2048 - NEAR)] * 2)
    far = swap(far, "zh")
    cuts = [(2, 128, NEAR), (2, 240, 1024)] * 2
    q0, q1, q2, q3 = kernel_of(cut_a, "cut_a", (early, late_a, first, second), cuts)
    q1, q3, q2 = shift(q1, "y", 1), shift(q3, "y", -1), shift(q2, "y", 2)

    (own,) = kernel_of(near_first, "near_first", (ab, ahead, behind), [(6, 128, 2048)], (q0,))
    own = own.reshape(768, 2048)
    parts = (early_mine, early_theirs, late_mine, late_theirs)
    grads = kernel_of(place_grads, "place_grads", parts, [(6, 128, 1152)] * 2 + [(2, 128, 1152)] * 2, (q0,))
    mine, theirs = (part.reshape(768, 1152) for part in grads[:2])
    mine_opposite, theirs_opposite = grads[2:]
    weight_grad = dot_tn(own, mine) + dot_tn(swap(own, "core"), theirs)

    waits = (q1, q2, q3, far, weight_grad)
    s0, s1, s2, s3 = kernel_of(sum_blocks, "sum_zh", (near, far), [(128, 2048 - NEAR)] * 4, waits)
    r1, r3, r2 = shift(s1, "y", 1), shift(s3, "y", -1), shift(s2, "y", 2)
    a0, a1 = kernel_of(sum_four, "sum_y", (q0, q1, q2, q3), [(128, NEAR)] * 2, waits)
    a1 = swap(a1, "zh")

    (own,) = kernel_of(opposite, "opposite", (q1, q3), [(2, 128, 2048)], (s1,))
    own, other = kernel_of(pair_up, "pair_up", (own, swap(own, "core"), mine_opposite, theirs_opposite), [(4, 128, 2048), (4, 128, 1152)])
    weight_grad += dot_tn(own.reshape(512, 2048), other.reshape(512, 1152))
    weight_grad = with_layout_constraint(weight_grad, Layout((0, 1)))

    parts = (a0, a1, s0, r1, r3, r2)
    (input_grad,) = kernel_of(sum_last, "sum_last", parts, [(128, 2048)], (weight_grad,))
    return input_grad, weight_grad


def solution(mesh):
    fine = Mesh(mesh.devices.reshape(SIZES), AXES)
    row, col = ("x", "zl"), ("zh", "y", "core")
    return jax.shard_map(
        on_device,
        mesh=fine,
        in_specs=(P(col, row), P(row, col), P(row, col)),
        out_specs=(P(col, row), P(row, col)),
        check_vma=False,
    )
```

```python
import jax
import jax.numpy as jnp
from jax import lax
from jax.experimental import pallas as pl
from jax.experimental.pallas import tpu as pltpu
from jax.experimental.layout import Layout, with_layout_constraint
from jax.sharding import Mesh
from jax.sharding import PartitionSpec as P

AXES = ("x", "zl", "zh", "y", "core")
SIZES = (4, 2, 2, 4, 2)


NEAR = 896
PACKED = [((slice(0, 64), slice(512 * i, 512 * i + 512)), (slice(64 * i, 64 * i + 64), slice(0, 512))) for i in range(2)]
PACKED += [((slice(64, 96), slice(256 * i, 256 * i + 256)), (slice(32 * i, 32 * i + 32), slice(512, 768))) for i in range(4)]
PACKED += [((slice(96, 112), slice(128 * i, 128 * i + 128)), (slice(16 * i, 16 * i + 16), slice(768, 896))) for i in range(8)]


def shift(value, axis, step):
    return lax.ppermute(value, axis, [(i, (i + step) % 4) for i in range(4)])


def swap(value, axis):
    return lax.ppermute(value, axis, [(0, 1), (1, 0)])


def after(value, *others):
    return lax.optimization_barrier((value, *others))[0]


def dot_nt(a, b):
    return lax.dot_general(a, b, (((1,), (1,)), ((), ())), preferred_element_type=jnp.float32)


def dot_tn(a, b):
    return lax.dot_general(a, b, (((0,), (0,)), ((), ())), preferred_element_type=jnp.float32)


def kernel_of(kernel, name, operands, shapes, waits=()):
    whole, anywhere = pl.BlockSpec(), pl.BlockSpec(memory_space=pl.ANY)
    n = len(operands)
    return pl.pallas_call(
        lambda *refs: kernel(*refs[:n], *refs[n + len(waits) :]),
        name=name,
        out_shape=[jax.ShapeDtypeStruct(shape, jnp.bfloat16) for shape in shapes],
        in_specs=[whole] * n + [anywhere] * len(waits),
        out_specs=[whole] * len(shapes),
        compiler_params=pltpu.CompilerParams(vmem_limit_bytes=16 * 2**20),
    )(*operands, *waits)


def distance(dx, dz):
    x, zl, zh, y = (lax.axis_index(axis) for axis in AXES[:4])
    bx, bz = (x + dx) & 3, zl ^ dz
    return zh ^ (bx >> 1), (((bx & 1) << 1) + bz - y) & 3


def by_core(*refs):
    core = lax.axis_index("core")
    for i, block in enumerate(refs[:4]):
        refs[4][i] = block[pl.ds(pl.multiple_of(core * 128, 128), 128)]
        refs[5][i] = block[pl.ds(pl.multiple_of(128 - core * 128, 128), 128)]


def place_grads(early_mine, early_theirs, late_mine, late_theirs, mine, theirs, mine_opposite, theirs_opposite):
    for late, part, other in ((0, early_mine, early_theirs), (1, late_mine, late_theirs)):
        for i in range(4):
            dz, dy = distance(i, late)

            @pl.when(dy == 2)
            def _():
                mine_opposite[dz] = part[i]
                theirs_opposite[dz] = other[i]

            @pl.when(dy != 2)
            def _():
                mine[dz * 3 + dy - (dy >> 1)] = part[i]
                theirs[dz * 3 + dy - (dy >> 1)] = other[i]


def cut_a(early, late, first, second, q0, q1, q2, q3):
    for is_late, part in ((0, early), (1, late)):
        for i in range(4):
            dz, dy = distance(i, is_late)
            for at, out in enumerate((q0, q1, q2, q3)):

                @pl.when(dy == at)
                def _():
                    if at % 2 == 0:
                        out[dz] = part[i, :, :NEAR]
                    else:
                        for there, here in PACKED:
                            out[dz, *there] = part[i, *here]

    for out, half in ((q1, first), (q3, second)):
        for dz in range(2):
            out[dz, 112:176] = half[dz, :, :1024]
            out[dz, 176:] = half[dz, :, 1024:]


def cut_b(early, late, near, far):
    for is_late, part, columns in ((0, early, slice(NEAR, 2048)), (1, late, slice(0, 2048 - NEAR))):
        for i in range(4):
            dz, dy = distance(i, is_late)
            for at, out in enumerate((near, far)):

                @pl.when(dz == at)
                def _():
                    out[dy] = part[i, :, columns]


def sum_blocks(first, second, *outs):
    for i, out in enumerate(outs):
        out[...] = (first[i].astype(jnp.float32) + second[i].astype(jnp.float32)).astype(jnp.bfloat16)


def sum_four(q0, q1, q2, q3, *outs):
    for i, out in enumerate(outs):
        for there, here in PACKED:
            total = q0[i, *here].astype(jnp.float32) + q2[i, *here].astype(jnp.float32)
            total += q1[i, *there].astype(jnp.float32) + q3[i, *there].astype(jnp.float32)
            out[here] = total.astype(jnp.bfloat16)


def sum_last(a0, a1, b0, b1, b2, b3, out):
    f32 = jnp.float32
    out[:, :NEAR] = (a0[...].astype(f32) + a1[...].astype(f32)).astype(jnp.bfloat16)
    total = b0[...].astype(f32) + b1[...].astype(f32) + b2[...].astype(f32) + b3[...].astype(f32)
    out[:, NEAR:] = total.astype(jnp.bfloat16)


def relay(block, out):
    out[...] = block[...]


def pair(a, b, out):
    out[0] = a[...]
    out[1] = b[...]


def halves(behind, ahead, first, second):
    first[...] = behind[:, :64]
    second[...] = ahead[:, 64:]


def near_first(ab, ahead, behind, out):
    for dz in range(2):
        for i, block in enumerate((ab, ahead, behind)):
            out[dz * 3 + i] = block[dz]


def opposite(behind, ahead, out):
    for rows, half in ((slice(0, 64), behind), (slice(64, 128), ahead)):
        for dz in range(2):
            out[dz, rows, :1024] = half[dz, 112:176]
            out[dz, rows, 1024:] = half[dz, 176:]


def pair_up(a0, a1, b0, b1, a, b):
    for out, parts in ((a, (a0, a1)), (b, (b0, b1))):
        for i, part in enumerate(parts):
            out[2 * i] = part[0]
            out[2 * i + 1] = part[1]


def on_device(inputs, weight, out_grad):
    bf16, f32 = jnp.bfloat16, jnp.float32

    g, h = out_grad, swap(out_grad, "zl")
    g2 = shift(g, "x", 2)

    (ab,) = kernel_of(pair, "pair", (inputs, swap(inputs, "zh")), [(2, 128, 2048)])
    (g,) = kernel_of(relay, "relay_g", (g,), [(256, 1152)], (g2, ab))
    g1, g3 = shift(g, "x", 1), shift(g, "x", -1)
    behind, ahead = shift(ab, "y", 1), shift(ab, "y", -1)
    first, second = kernel_of(halves, "halves", (behind, ahead), [(2, 64, 2048)] * 2)

    (h,) = kernel_of(relay, "relay", (h,), [(256, 1152)], (ab, g1))
    h1, h3, h2 = shift(h, "x", 1), shift(h, "x", -1), swap(g2, "zl")
    wa, wb = weight[:NEAR], weight[NEAR:]
    blocks = [(4, 128, 1152)] * 2
    early_mine, early_theirs = kernel_of(by_core, "by_core_early", (g, g3, g2, g1), blocks)

    def theirs_of(part, w):
        return dot_nt(part.reshape(512, 1152), w).astype(bf16)

    def partial(part, w, other):
        return (dot_nt(part.reshape(512, 1152), w) + other.astype(f32)).astype(bf16).reshape(4, 128, -1)

    early = partial(early_mine, weight, swap(theirs_of(early_theirs, weight), "core"))
    late_mine, late_theirs = kernel_of(by_core, "by_core_late", (h, h3, h2, h1), blocks, (first,))
    late_b = theirs_of(late_theirs, wb)
    late_a = theirs_of(after(late_theirs, late_b), wa)
    late_b = partial(late_mine, wb, swap(late_b, "core"))
    late_a = partial(after(late_mine, late_b), wa, swap(late_a, "core"))
    near, far = kernel_of(cut_b, "cut_b", (early, late_b), [(4, 128, 2048 - NEAR)] * 2)
    far = swap(far, "zh")
    cuts = [(2, 128, NEAR), (2, 240, 1024)] * 2
    q0, q1, q2, q3 = kernel_of(cut_a, "cut_a", (early, late_a, first, second), cuts)
    q1, q3, q2 = shift(q1, "y", 1), shift(q3, "y", -1), shift(q2, "y", 2)

    (own,) = kernel_of(near_first, "near_first", (ab, ahead, behind), [(6, 128, 2048)], (q0,))
    own = own.reshape(768, 2048)
    parts = (early_mine, early_theirs, late_mine, late_theirs)
    grads = kernel_of(place_grads, "place_grads", parts, [(6, 128, 1152)] * 2 + [(2, 128, 1152)] * 2, (q0,))
    mine, theirs = (part.reshape(768, 1152) for part in grads[:2])
    mine_opposite, theirs_opposite = grads[2:]
    weight_grad = dot_tn(own, mine) + dot_tn(swap(own, "core"), theirs)

    waits = (q1, q2, q3, far, weight_grad)
    s0, s1, s2, s3 = kernel_of(sum_blocks, "sum_zh", (near, far), [(128, 2048 - NEAR)] * 4, (q2, weight_grad))
    r1, r3, r2 = shift(s1, "y", 1), shift(s3, "y", -1), shift(s2, "y", 2)
    a0, a1 = kernel_of(sum_four, "sum_y", (q0, q1, q2, q3), [(128, NEAR)] * 2, waits)
    a1 = swap(a1, "zh")

    (own,) = kernel_of(opposite, "opposite", (q1, q3), [(2, 128, 2048)], (s1,))
    own, other = kernel_of(pair_up, "pair_up", (own, swap(own, "core"), mine_opposite, theirs_opposite), [(4, 128, 2048), (4, 128, 1152)])
    weight_grad += dot_tn(own.reshape(512, 2048), other.reshape(512, 1152))
    weight_grad = with_layout_constraint(weight_grad, Layout((0, 1)))

    parts = (a0, a1, s0, r1, r3, r2)
    (input_grad,) = kernel_of(sum_last, "sum_last", parts, [(128, 2048)], (weight_grad,))
    return input_grad, weight_grad


def solution(mesh):
    fine = Mesh(mesh.devices.reshape(SIZES), AXES)
    row, col = ("x", "zl"), ("zh", "y", "core")
    return jax.shard_map(
        on_device,
        mesh=fine,
        in_specs=(P(col, row), P(row, col), P(row, col)),
        out_specs=(P(col, row), P(row, col)),
        check_vma=False,
    )
```
